256 devices in a mesh: row: 32 (over y, z), col: 8 (over x, core).
Axes of the slice: x: 4, y: 4, z: 8, core: 2. Of those that a mesh axis runs over, the one named last changes fastest.
Arguments:
- context: bfloat16 [262144, 512], P(('row', 'col')), may hold values from -6 to 6
- cotangent: bfloat16 [262144, 1024], P(('row', 'col')), may hold values from -0.1875 to 0.1875
- out_weight: bfloat16 [512, 1024], replicated, may hold values from -0.1875 to 0.1875
- momentum: float32 [512, 1024], replicated, may hold values from -6 to 6
- worker_error: float32 [32, 8, 32, 16384], P('row', 'col'), may hold values from -3 to 3
- server_rows: float32 [32, 8, 32, 512], P('row', 'col'), may hold values from -3 to 3
- server_cols: float32 [32, 8, 32, 64], P('row', 'col'), may hold values from -3 to 3
Outputs:
- input_grad: bfloat16 [262144, 512], P(('row', 'col'))
- average: float32 [512, 1024], replicated
- worker_new: float32 [32, 8, 32, 16384], P('row', 'col')
- rows_new: float32 [32, 8, 32, 512], P('row', 'col')
- cols_new: float32 [32, 8, 32, 64], P('row', 'col')
The draws below stay inside these ranges and needn't reach their ends.
All inputs are finite; a program needn't handle non-finite values.
Results may differ from the reference program's by a relative error of at most 0.025.
Values may be sent and summed in bfloat16 or wider, within the bound.
A program may use at most 64 MiB of HBM per device.

```python
import jax
import jax.numpy as jnp
from jax import lax

D = 1024
INW = 512
TOK_DEV = 1024
TOKENS = 262144
COLS = 16384
N_ROW = 32
N_COL = 8


def steps_of(rng, dims, cuts, low, largest):
    def one(dim, shards_of):
        steps = jax.random.uniform(jax.random.fold_in(jax.random.fold_in(rng, 6), dim), (shards_of,), jnp.float32, low / len(cuts), largest / len(cuts))
        return jnp.repeat(jnp.exp(steps), dims[dim] // shards_of).reshape((-1,) + (1,) * (len(dims) - dim - 1))

    factor_of = one(*cuts[0])
    for cut in cuts[1:]:
        factor_of = factor_of * one(*cut)
    return factor_of


def gaussian(own_key, dims, scale, reach, shards=(), dtype=jnp.bfloat16):
    level = steps_of(own_key, dims, shards, -0.22, 0.18) if shards else 1.0
    result = jax.random.normal(own_key, dims, jnp.float32) * scale * level
    return jnp.minimum(jnp.maximum(result, -reach), reach).astype(dtype)


def setup_inputs(seed: int = 0) -> dict:
    keys = jax.random.split(jax.random.key(seed), 8)
    return {
        "context": gaussian(keys[0], (TOKENS, INW), 1.0, 6.0, ((0, 256),)),
        "cotangent": gaussian(keys[1], (TOKENS, D), TOK_DEV ** -0.5, 0.1875, ((0, 256),)),
        "out_weight": gaussian(keys[2], (INW, D), D ** -0.5, 0.1875),
        "momentum": gaussian(keys[3], (INW, D), 1.0, 6.0, (), jnp.float32),
        "worker_error": gaussian(keys[4], (N_ROW, N_COL, 32, COLS), 0.3, 3.0, ((0, 32), (1, 8)), jnp.float32),
        "server_rows": gaussian(keys[5], (N_ROW, N_COL, 32, COLS // N_ROW), 0.3, 3.0, ((0, 32), (1, 8)), jnp.float32),
        "server_cols": gaussian(keys[6], (N_ROW, N_COL, 32, COLS // (N_ROW * N_COL)), 0.3, 3.0, ((0, 32), (1, 8)), jnp.float32),
    }


def compress(values):
    scale = jnp.sqrt(lax.optimization_barrier(jnp.mean(values * values, axis=(-2, -1), keepdims=True)) + 1e-06)
    packed = (scale * jnp.tanh(3.0 * values / scale)).astype(jnp.bfloat16)
    return (packed, values - packed.astype(jnp.float32))

def reference(context, cotangent, out_weight, momentum, worker_error, server_rows, server_cols):
    lanes = worker_error.shape[2]
    width = worker_error.shape[3]
    block = width // N_ROW
    piece = block // N_COL
    input_grad = lax.dot_general(cotangent, out_weight, (((1,), (1,)), ((), ())), preferred_element_type=jnp.float32).astype(jnp.bfloat16)
    ctx_all = context.reshape(N_ROW, N_COL, TOK_DEV, INW).astype(jnp.float32)
    cot_all = cotangent.reshape(N_ROW, N_COL, TOK_DEV, D).astype(jnp.float32)
    grad = jnp.einsum('rctk,rctd->rckd', ctx_all, cot_all, precision=lax.Precision.HIGHEST)
    values = (0.9 * momentum + 0.1 * grad).reshape(N_ROW, N_COL, lanes, width) + worker_error
    sent, worker_new = compress(values)
    blocks = sent.astype(jnp.float32).reshape(N_ROW, N_COL, lanes, N_ROW, block)
    first = jnp.transpose(lax.optimization_barrier(jnp.sum(blocks, axis=0)), (2, 0, 1, 3)) / N_ROW + server_rows
    middle, rows_new = compress(first)
    pieces = middle.astype(jnp.float32).reshape(N_ROW, N_COL, lanes, N_COL, piece)
    second = jnp.transpose(lax.optimization_barrier(jnp.sum(pieces, axis=1)), (0, 2, 1, 3)) / N_COL + server_cols
    final, cols_new = compress(second)
    average = jnp.transpose(final, (2, 0, 1, 3)).reshape(lanes, width).astype(jnp.float32).reshape(INW, D)
    return (input_grad, average, worker_new, rows_new, cols_new)
```

```python
import functools

import jax
import jax.numpy as jnp
from jax import lax
from jax.experimental import pallas as pl
from jax.experimental.pallas import tpu as pltpu
from jax.sharding import PartitionSpec as P

MESH = pl.DeviceIdType.MESH
F32, BF16 = jnp.float32, jnp.bfloat16

NX, NY, NZ, NC = 4, 4, 8, 2
LANES, WIDTH = 32, 16384
BLOCK = 512
YC = 384
ZC = BLOCK - YC
ROWS = 16


def place():
    row, col = lax.axis_index("row"), lax.axis_index("col")
    return col // NC, row // NZ, lax.rem(row, NZ), lax.rem(col, NC)


def device(x, y, z, c):
    return (y * NZ + z, x * NC + c)


def scale_of(total, count):
    return jnp.sqrt(total / count + 1e-06)


def total_of(values):
    return jnp.sum(jnp.sum(values, axis=0, keepdims=True), axis=1, keepdims=True)


def compress(values):
    scale = scale_of(total_of(values * values), values.size)
    packed = (scale * jnp.tanh(values * (3.0 / scale))).astype(BF16)
    return packed, values - packed.astype(F32)


def partners():
    found = [(0, d, 0, 0) for d in range(1, NY)]
    found += [(0, 0, d, 0) for d in range(1, NZ)]
    found += [(dx, 0, 0, dc) for dx in range(NX) for dc in range(NC) if dx or dc]
    found += [(dx, dy, 0, 0) for dx in range(1, NX) for dy in range(1, NY)]
    return found


def fused(
    ctx_h, cot_h, w_h, mom_h, we_h, sr_h, sc_h,
    g_h, wn_h, ig_h, rn_h, cn_h,
    ctx, cot, w, mom, we, sr, sc, ctx_t, grad, vals, ig, rn, cn,
    send_y, got_y, send_z, got_z, part_y, got_y2, part_z, got_z2,
    mid, got_c, fin, gat,
    in_sem, out_sem, wn_sem,
    y_s, y_r, z_s, z_r, y2_s, y2_r, z2_s, z2_r, c_s, c_r, f_s, f_r, p_s, p_r, b_s, b_r,
):
    x, y, z, c = place()

    barrier = pltpu.get_barrier_semaphore()
    known = partners()
    for dx, dy, dz, dc in known:
        there = device(lax.rem(x + dx, NX), lax.rem(y + dy, NY), lax.rem(z + dz, NZ), lax.rem(c + dc, NC))
        pl.semaphore_signal(barrier, inc=1, device_id=there, device_id_type=MESH)

    loads = [
        pltpu.make_async_copy(src, dst, in_sem.at[i])
        for i, (src, dst) in enumerate(
            [(ctx_h, ctx), (cot_h, cot), (w_h, w), (we_h.at[0, 0], we), (sr_h.at[0, 0], sr), (sc_h.at[0, 0], sc)]
            + [(mom_h.at[:, pl.ds(128 * k, 128)], mom.at[k]) for k in range(8)]
        )
    ]
    for load in loads:
        load.start()

    loads[0].wait()
    ctx_t[...] = ctx[...].T
    loads[1].wait()

    @pl.loop(0, 4)
    def _(n):
        cols = pl.ds(pl.multiple_of(n * 256, 256), 256)
        product = jnp.dot(ctx_t[...], cot[:, cols], preferred_element_type=F32)
        grad[2 * n] = product[:, :128]
        grad[2 * n + 1] = product[:, 128:]

    for load in loads[3:4] + loads[6:]:
        load.wait()

    def accumulate(q, total):
        rows = pl.ds(q, LANES, stride=ROWS)
        for k in range(8):
            cols = pl.ds(pl.multiple_of(q * 1024 + 128 * k, 128), 128)
            v = 0.9 * mom[k, rows, :] + 0.1 * grad[k, rows, :] + we[:, cols]
            vals[q, :, 128 * k : 128 * k + 128] = v
            v = v * v
            total = total + (v[0:8] + v[8:16]) + (v[16:24] + v[24:32])
        return total

    total = lax.fori_loop(0, ROWS, accumulate, jnp.zeros((8, 128), F32))
    scale = scale_of(total_of(total), LANES * WIDTH)
    slope = 3.0 / scale

    def soft(v):
        return (scale * jnp.tanh(v * slope)).astype(BF16)

    @pl.loop(0, ROWS)
    def _(q):
        for half in range(2):
            b = 2 * q + half
            cols = pl.ds(half * BLOCK + YC, ZC)
            v = vals[q, :, cols]
            p = soft(v)
            send_z[lax.rem(b, NZ), b // NZ] = p
            vals[q, :, cols] = v - p.astype(F32)

    pl.semaphore_wait(barrier, len(known))

    z_copies = []
    for d in (4, 3, 5, 2, 6, 1, 7):
        to = lax.rem(z + d, NZ)
        copy = pltpu.make_async_remote_copy(
            src_ref=send_z.at[to], dst_ref=got_z.at[z], send_sem=z_s.at[d], recv_sem=z_r.at[d],
            device_id=device(x, y, to, c), device_id_type=MESH,
        )
        copy.start()
        z_copies.append(copy)
    got_z[z] = send_z[z]

    y_copies, wn_copies = {}, []
    for e in (2, 1, 3, 0):
        k = lax.rem(z // 2 + e, NZ // 2)
        for d in (2, 1, 3, 0):
            to = lax.rem(y + d, NY)
            q = to * 4 + k
            for half in range(2):
                cols = pl.ds(half * BLOCK, YC)
                v = vals[q, :, cols]
                p = soft(v)
                if d:
                    send_y[to, 2 * k + half] = p
                else:
                    got_y[y, 2 * k + half] = p
                vals[q, :, cols] = v - p.astype(F32)
            if d:
                pair = pl.ds(2 * k, 2)
                copy = pltpu.make_async_remote_copy(
                    src_ref=send_y.at[to, pair], dst_ref=got_y.at[y, pair], send_sem=y_s.at[e, d], recv_sem=y_r.at[e, d],
                    device_id=device(x, to, z, c), device_id_type=MESH,
                )
                copy.start()
                y_copies[e, d] = copy
            copy = pltpu.make_async_copy(
                vals.at[q], wn_h.at[:, pl.ds(pl.multiple_of(q * 1024, 1024), 1024)], wn_sem.at[4 * e + d]
            )
            copy.start()
            wn_copies.append(copy)

    loads[2].wait()

    @pl.loop(0, 4)
    def _(n):
        rows = pl.ds(pl.multiple_of(n * 256, 256), 256)
        ig[rows, :] = lax.dot_general(
            cot[rows, :], w[...], (((1,), (1,)), ((), ())), preferred_element_type=F32
        ).astype(BF16)

    ig_copy = pltpu.make_async_copy(ig, ig_h, out_sem.at[0])
    ig_copy.start()

    def add(parts):
        total = parts[0].astype(F32)
        for part in parts[1:]:
            total = total + part.astype(F32)
        return total

    y2_copies = []

    def send_part(to):
        d = lax.rem(to - z + NZ, NZ)
        copy = pltpu.make_async_remote_copy(
            src_ref=part_y.at[to], dst_ref=got_y2.at[z], send_sem=y2_s.at[d], recv_sem=y2_r.at[d],
            device_id=device(x, y, to, c), device_id_type=MESH,
        )
        copy.start()
        y2_copies.append(copy)

    def sum_y(at):
        return add([got_y[i, at] for i in range(NY)]).astype(BF16)

    for e in (2, 1, 3):
        for d in (2, 1, 3):
            y_copies[e, d].wait_recv()
        k = lax.rem(z // 2 + e, NZ // 2)
        for half in range(2):
            part_y[2 * k + half] = sum_y(2 * k + half)
            send_part(2 * k + half)

    for copy in z_copies:
        copy.wait_recv()
    z2_copies = []
    for d in (2, 1, 3, 0):
        to = lax.rem(y + d, NY)
        part = add([got_z[i, to] for i in range(NZ)]).astype(BF16)
        if d:
            part_z[to] = part
            copy = pltpu.make_async_remote_copy(
                src_ref=part_z.at[to], dst_ref=got_z2.at[y], send_sem=z2_s.at[d], recv_sem=z2_r.at[d],
                device_id=device(x, to, z, c), device_id_type=MESH,
            )
            copy.start()
            z2_copies.append(copy)
        else:
            got_z2[y] = part

    for d in (2, 1, 3):
        y_copies[0, d].wait_recv()
    other = z + 1 - 2 * lax.rem(z, 2)
    part_y[other] = sum_y(other)
    send_part(other)
    got_y2[z] = sum_y(z)

    loads[4].wait()
    loads[5].wait()
    for copy in z2_copies:
        copy.wait_recv()
    for d in (4, 3, 5, 2, 6, 1, 7):
        pltpu.make_async_remote_copy(
            src_ref=part_y.at[0], dst_ref=got_y2.at[0], send_sem=y2_s.at[d], recv_sem=y2_r.at[d],
            device_id=device(x, y, lax.rem(z + d, NZ), c), device_id_type=MESH,
        ).wait_recv()
    first = jnp.concatenate(
        [add([got_y2[i] for i in range(NZ)]), add([got_z2[i] for i in range(NY)])], axis=1
    ) * (1.0 / (NY * NZ)) + sr[...]
    middle, rest = compress(first)

    low = lax.broadcasted_iota(jnp.int32, (ROWS, 128), 1) < 64

    def fold(top, bottom):
        return (
            jnp.where(low, top, pltpu.roll(bottom, 64, axis=1)),
            jnp.where(low, pltpu.roll(top, 64, axis=1), bottom),
        )

    middle = middle.astype(F32)
    for k in range(NX):
        group = middle[:, 128 * k : 128 * k + 128]
        even, odd = fold(group[:16], group[16:])
        mid[2 * k] = even.astype(BF16)
        mid[2 * k + 1] = odd.astype(BF16)
    c_copies = []
    for dx in (2, 1, 3, 0):
        for dc in range(NC):
            if dx or dc:
                tx, tc = lax.rem(x + dx, NX), lax.rem(c + dc, NC)
                copy = pltpu.make_async_remote_copy(
                    src_ref=mid.at[2 * tx + tc], dst_ref=got_c.at[2 * x + c],
                    send_sem=c_s.at[2 * dx + dc], recv_sem=c_r.at[2 * dx + dc],
                    device_id=device(tx, y, z, tc), device_id_type=MESH,
                )
                copy.start()
                c_copies.append(copy)
    got_c[2 * x + c] = mid[2 * x + c]
    rn[...] = rest
    rn_copy = pltpu.make_async_copy(rn, rn_h, out_sem.at[1])
    rn_copy.start()
    side = jnp.concatenate([sc[0:16, :], sc[16:32, :]], axis=1)
    for copy in c_copies:
        copy.wait_recv()
    second = add([got_c[i] for i in range(NX * NC)]) * (1.0 / (NX * NC)) + side
    final, rest = compress(second)

    fin[...] = final
    f_copies = []
    for d in (4, 3, 5, 2, 6, 1, 7):
        copy = pltpu.make_async_remote_copy(
            src_ref=fin, dst_ref=gat.at[c, y, x, z], send_sem=f_s.at[d], recv_sem=f_r.at[d],
            device_id=device(x, y, lax.rem(z + d, NZ), c), device_id_type=MESH,
        )
        copy.start()
        f_copies.append(copy)
    gat[c, y, x, z] = final
    cn[0:16, :] = rest[:, 0:64]
    cn[16:32, :] = pltpu.roll(rest, 64, axis=1)[:, 0:64]
    cn_copy = pltpu.make_async_copy(cn, cn_h, out_sem.at[2])
    cn_copy.start()
    for copy in f_copies:
        copy.wait_recv()

    p_copies, b_copies = [], []

    def to_sibling(dx, dy):
        sx, sy = lax.rem(x - dx + NX, NX), lax.rem(y - dy + NY, NY)
        copy = pltpu.make_async_remote_copy(
            src_ref=gat.at[c, sy, sx], dst_ref=gat.at[c, sy, sx],
            send_sem=b_s.at[dx, dy], recv_sem=b_r.at[dx, dy],
            device_id=device(x, y, z, 1 - c), device_id_type=MESH,
        )
        copy.start()
        b_copies.append(copy)

    order = sorted(
        [(dx, dy) for dx in range(NX) for dy in range(NY) if dx or dy],
        key=lambda d: -(min(d[0], NX - d[0]) + min(d[1], NY - d[1])),
    )
    for dx, dy in order:
        copy = pltpu.make_async_remote_copy(
            src_ref=gat.at[c, y, x], dst_ref=gat.at[c, y, x],
            send_sem=p_s.at[dx, dy], recv_sem=p_r.at[dx, dy],
            device_id=device(lax.rem(x + dx, NX), lax.rem(y + dy, NY), z, c), device_id_type=MESH,
        )
        copy.start()
        p_copies.append(((dx, dy), copy))
    to_sibling(0, 0)
    for (dx, dy), copy in reversed(p_copies):
        copy.wait_recv()
        to_sibling(dx, dy)
    for copy in b_copies:
        copy.wait_recv()
    g_copy = pltpu.make_async_copy(gat, g_h, out_sem.at[3])
    g_copy.start()

    for copy in z_copies + list(y_copies.values()) + z2_copies + y2_copies + c_copies + f_copies + b_copies:
        copy.wait_send()
    for _, copy in p_copies:
        copy.wait_send()
    for copy in wn_copies + [ig_copy, rn_copy, cn_copy, g_copy]:
        copy.wait()


def finish(g, wn, ig, rn, cn, avg, wn_out, ig_out, rn_out, cn_out):
    low = lax.broadcasted_iota(jnp.int32, (ROWS, 128), 1) < 64
    for y in range(NY):
        for h in range(NZ // 2):
            even = g[0, y, 0, h, 0].astype(F32)
            odd = g[1, y, 0, h, 0].astype(F32)
            q = y * 4 + h
            avg[pl.ds(q, 16, stride=ROWS), :] = jnp.where(low, even, pltpu.roll(odd, 64, axis=1))
            avg[pl.ds(256 + q, 16, stride=ROWS), :] = jnp.where(low, pltpu.roll(even, 64, axis=1), odd)
    wn_out[0, 0] = wn[...]
    ig_out[...] = ig[...]
    rn_out[0, 0] = rn[...]
    cn_out[0, 0] = cn[...]


def local(context, cotangent, out_weight, momentum, worker_error, server_rows, server_cols):
    anywhere = pl.BlockSpec(memory_space=pl.ANY)
    dma = pltpu.SemaphoreType.DMA
    g, wn, ig, rn, cn = pl.pallas_call(
        fused,
        out_shape=(
            jax.ShapeDtypeStruct((NC, NY, NX, NZ, 16, 128), BF16),
            jax.ShapeDtypeStruct((LANES, WIDTH), F32),
            jax.ShapeDtypeStruct((1024, 512), BF16),
            jax.ShapeDtypeStruct((LANES, BLOCK), F32),
            jax.ShapeDtypeStruct((LANES, 64), F32),
        ),
        in_specs=[pl.BlockSpec(memory_space=pltpu.HBM)] * 7,
        out_specs=[anywhere] * 5,
        scratch_shapes=[
            pltpu.VMEM((1024, 512), BF16),
            pltpu.VMEM((1024, 1024), BF16),
            pltpu.VMEM((512, 1024), BF16),
            pltpu.VMEM((8, 512, 128), F32),
            pltpu.VMEM((LANES, WIDTH), F32),
            pltpu.VMEM((LANES, BLOCK), F32),
            pltpu.VMEM((LANES, 64), F32),
            pltpu.VMEM((512, 1024), BF16),
            pltpu.VMEM((8, 512, 128), F32),
            pltpu.VMEM((ROWS, LANES, 1024), F32),
            pltpu.VMEM((1024, 512), BF16),
            pltpu.VMEM((LANES, BLOCK), F32),
            pltpu.VMEM((LANES, 64), F32),
            pltpu.VMEM((NY, NZ, LANES, YC), BF16),
            pltpu.VMEM((NY, NZ, LANES, YC), BF16),
            pltpu.VMEM((NZ, NY, LANES, ZC), BF16),
            pltpu.VMEM((NZ, NY, LANES, ZC), BF16),
            pltpu.VMEM((NZ, LANES, YC), BF16),
            pltpu.VMEM((NZ, LANES, YC), BF16),
            pltpu.VMEM((NY, LANES, ZC), BF16),
            pltpu.VMEM((NY, LANES, ZC), BF16),
            pltpu.VMEM((NX * NC, 16, 128), BF16),
            pltpu.VMEM((NX * NC, 16, 128), BF16),
            pltpu.VMEM((16, 128), BF16),
            pltpu.VMEM((NC, NY, NX, NZ, 16, 128), BF16),
            dma((14,)), dma((4,)), dma((16,)),
            dma((4, NY)), dma((4, NY)), dma((NZ,)), dma((NZ,)),
            dma((NZ,)), dma((NZ,)), dma((NY,)), dma((NY,)),
            dma((NX * NC,)), dma((NX * NC,)), dma((NZ,)), dma((NZ,)),
            dma((NX, NY)), dma((NX, NY)), dma((NX, NY)), dma((NX, NY)),
        ],
        compiler_params=pltpu.CompilerParams(
            collective_id=0, has_side_effects=True, vmem_limit_bytes=60 << 20
        ),
        cost_estimate=pl.CostEstimate(flops=2 << 30, bytes_accessed=13 << 20, transcendentals=1 << 19),
        name="fused",
    )(context, cotangent, out_weight, momentum, worker_error, server_rows, server_cols)
    return pl.pallas_call(
        finish,
        grid=(8,),
        out_shape=(
            jax.ShapeDtypeStruct((512, 1024), F32),
            jax.ShapeDtypeStruct((1, 1, LANES, WIDTH), F32),
            jax.ShapeDtypeStruct((1024, 512), BF16),
            jax.ShapeDtypeStruct((1, 1, LANES, BLOCK), F32),
            jax.ShapeDtypeStruct((1, 1, LANES, 64), F32),
        ),
        in_specs=[
            pl.BlockSpec((NC, NY, 1, NZ // 2, 1, 16, 128), lambda j: (0, 0, lax.rem(j, 4), 0, j // 4, 0, 0)),
            pl.BlockSpec((LANES, WIDTH // 8), lambda j: (0, j)),
            pl.BlockSpec((128, 512), lambda j: (j, 0)),
            pl.BlockSpec((LANES, 128), lambda j: (0, j // 2)),
            pl.BlockSpec((LANES, 64), lambda j: (0, 0)),
        ],
        out_specs=[
            pl.BlockSpec((512, 128), lambda j: (0, j)),
            pl.BlockSpec((1, 1, LANES, WIDTH // 8), lambda j: (0, 0, 0, j)),
            pl.BlockSpec((128, 512), lambda j: (j, 0)),
            pl.BlockSpec((1, 1, LANES, 128), lambda j: (0, 0, 0, j // 2)),
            pl.BlockSpec((1, 1, LANES, 64), lambda j: (0, 0, 0, 0)),
        ],
        compiler_params=pltpu.CompilerParams(vmem_limit_bytes=60 << 20),
        cost_estimate=pl.CostEstimate(flops=1 << 20, bytes_accessed=9 << 20, transcendentals=0),
        name="finish",
    )(g.reshape(NC, NY, NX, NZ // 2, 2, 16, 128), wn, ig, rn, cn)


def solution(mesh):
    state = P("row", "col", None, None)
    tokens = P(("row", "col"), None)

    def body(*args):
        avg, wn, ig, rn, cn = local(*args)
        return ig, avg, wn, rn, cn

    return jax.shard_map(
        body,
        mesh=mesh,
        in_specs=(tokens, tokens, P(), P(), state, state, state),
        out_specs=(tokens, P(), state, state, state),
        check_vma=False,
    )
```

```python
import functools

import jax
import jax.numpy as jnp
from jax import lax
from jax.experimental import pallas as pl
from jax.experimental.pallas import tpu as pltpu
from jax.sharding import PartitionSpec as P

MESH = pl.DeviceIdType.MESH
F32, BF16 = jnp.float32, jnp.bfloat16

NX, NY, NZ, NC = 4, 4, 8, 2
LANES, WIDTH = 32, 16384
BLOCK = 512
YC = 384
ZC = BLOCK - YC
ROWS = 16


def place():
    row, col = lax.axis_index("row"), lax.axis_index("col")
    return col // NC, row // NZ, lax.rem(row, NZ), lax.rem(col, NC)


def device(x, y, z, c):
    return (y * NZ + z, x * NC + c)


def scale_of(total, count):
    return jnp.sqrt(total / count + 1e-06)


def total_of(values):
    return jnp.sum(jnp.sum(values, axis=0, keepdims=True), axis=1, keepdims=True)


def compress(values):
    scale = scale_of(total_of(values * values), values.size)
    packed = (scale * jnp.tanh(values * (3.0 / scale))).astype(BF16)
    return packed, values - packed.astype(F32)


def partners():
    found = [(0, d, 0, 0) for d in range(1, NY)]
    found += [(0, 0, d, 0) for d in range(1, NZ)]
    found += [(dx, 0, 0, dc) for dx in range(NX) for dc in range(NC) if dx or dc]
    found += [(dx, dy, 0, 0) for dx in range(1, NX) for dy in range(1, NY)]
    return found


def fused(
    ctx_h, cot_h, w_h, mom_h, we_h, sr_h, sc_h,
    avg_h, wn_h, ig_h, rn_h, cn_h,
    ctx, cot, w, mom, we, sr, sc, ctx_t, grad, avg, vals, ig, rn, cn,
    send_y, got_y, send_z, got_z, part_y, got_y2, part_z, got_z2, mid, got_c, fin, gat, interleave, pieces,
    in_sem, out_sem, y_s, y_r, z_s, z_r, y2_s, y2_r, z2_s, z2_r, m_s, m_r, f_s, f_r, p_s, p_r, t_s, t_r,
):
    x, y, z, c = place()

    barrier = pltpu.get_barrier_semaphore()
    known = partners()
    for dx, dy, dz, dc in known:
        there = device(lax.rem(x + dx, NX), lax.rem(y + dy, NY), lax.rem(z + dz, NZ), lax.rem(c + dc, NC))
        pl.semaphore_signal(barrier, inc=1, device_id=there, device_id_type=MESH)

    loads = [
        pltpu.make_async_copy(src, dst, in_sem.at[i])
        for i, (src, dst) in enumerate(
            [(ctx_h, ctx), (cot_h, cot), (we_h.at[0, 0], we)]
            + [(mom_h.at[:, pl.ds(128 * k, 128)], mom.at[k]) for k in range(8)]
            + [(w_h, w), (sr_h.at[0, 0], sr), (sc_h.at[0, 0], sc)]
        )
    ]
    for load in loads:
        load.start()

    a = lax.broadcasted_iota(jnp.int32, (256, 256), 0)
    b = lax.broadcasted_iota(jnp.int32, (256, 256), 1)
    interleave[...] = jnp.where(b == lax.rem(a, ROWS) * ROWS + a // ROWS, 1.0, 0.0).astype(BF16)

    loads[0].wait()
    ctx_t[...] = ctx[...].T
    loads[1].wait()

    @pl.loop(0, 4)
    def _(n):
        cols = pl.ds(pl.multiple_of(n * 256, 256), 256)
        product = jnp.dot(ctx_t[...], cot[:, cols], preferred_element_type=F32)
        grad[2 * n] = product[:, :128]
        grad[2 * n + 1] = product[:, 128:]

    total = jnp.zeros((8, 128), F32)
    loads[2].wait()
    for k in range(8):
        loads[3 + k].wait()
        for q in range(ROWS):
            rows = pl.ds(q, LANES, stride=ROWS)
            v = 0.9 * mom[k, rows, :] + 0.1 * grad[k, rows, :] + we[:, 1024 * q + 128 * k : 1024 * q + 128 * k + 128]
            vals[q, :, 128 * k : 128 * k + 128] = v
            v = v * v
            total = total + ((v[0:8] + v[8:16]) + (v[16:24] + v[24:32]))
    scale = scale_of(total_of(total), LANES * WIDTH)
    slope = 3.0 / scale

    def soft(v):
        return (scale * jnp.tanh(v * slope)).astype(BF16)

    pl.semaphore_wait(barrier, len(known))

    def remote(src, dst, sems, at, to):
        copy = pltpu.make_async_remote_copy(
            src_ref=src, dst_ref=dst, send_sem=sems[0].at[at], recv_sem=sems[1].at[at],
            device_id=device(*to), device_id_type=MESH,
        )
        copy.start()
        return copy

    outs = []

    def keep(src, dst):
        copy = pltpu.make_async_copy(src, dst, out_sem.at[len(outs)])
        copy.start()
        outs.append(copy)

    def add(parts):
        total = parts[0].astype(F32)
        for one in parts[1:]:
            total = total + one.astype(F32)
        return total

    order = (2, 1, 3, 0)
    y_copies, z_copies = {}, []

    def along_z(to):
        d = lax.rem(to - z + NZ, NZ)
        z_copies.append(remote(send_z.at[to], got_z.at[z], (z_s, z_r), d, (x, y, to, c)))

    for e in order:
        k = lax.rem(z // 2 + e, NZ // 2)
        for d in order:
            to = lax.rem(y + d, NY)
            q = to * 4 + k
            for half in range(2):
                cols = pl.ds(half * BLOCK, BLOCK)
                v = vals[q, :, cols]
                p = soft(v)
                if d:
                    send_y[to, 2 * k + half] = p[:, :YC]
                else:
                    got_y[y, 2 * k + half] = p[:, :YC]
                send_z[2 * k + half, to] = p[:, YC:]
                vals[q, :, cols] = v - p.astype(F32)
            if d:
                pair = pl.ds(2 * k, 2)
                y_copies[e, d] = remote(
                    send_y.at[to, pair], got_y.at[y, pair], (y_s, y_r), (e, d), (x, to, z, c)
                )
        if e:
            along_z(2 * k)
            along_z(2 * k + 1)
    other = z + 1 - 2 * lax.rem(z, 2)
    along_z(other)
    got_z[z] = send_z[z]
    keep(vals, wn_h)

    y2_copies, z2_copies = [], []

    def sum_y(at):
        return add([got_y[i, at] for i in range(NY)]).astype(BF16)

    def send_part(to):
        part_y[to] = sum_y(to)
        d = lax.rem(to - z + NZ, NZ)
        y2_copies.append(remote(part_y.at[to], got_y2.at[z], (y2_s, y2_r), d, (x, y, to, c)))

    for e in (2, 1, 3):
        for d in (2, 1, 3):
            y_copies[e, d].wait_recv()
        k = lax.rem(z // 2 + e, NZ // 2)
        send_part(2 * k)
        send_part(2 * k + 1)

    far_first = (4, 3, 5, 2, 6, 1, 7)

    def from_z(sems, d, block):
        pltpu.make_async_remote_copy(
            src_ref=block, dst_ref=block, send_sem=sems[0].at[d], recv_sem=sems[1].at[d],
            device_id=device(x, y, lax.rem(z + d, NZ), c), device_id_type=MESH,
        ).wait_recv()

    for d in (2, 1, 3):
        y_copies[0, d].wait_recv()
    send_part(other)
    got_y2[z] = sum_y(z)
    for d in far_first:
        from_z((z_s, z_r), d, got_z.at[0])
    for d in order:
        to = lax.rem(y + d, NY)
        total = add([got_z[i, to] for i in range(NZ)]).astype(BF16)
        if d:
            part_z[to] = total
            z2_copies.append(remote(part_z.at[to], got_z2.at[y], (z2_s, z2_r), d, (x, to, z, c)))
        else:
            got_z2[y] = total

    loads[12].wait()
    loads[13].wait()
    for copy in z2_copies:
        copy.wait_recv()
    for d in far_first:
        from_z((y2_s, y2_r), d, got_y2.at[0])
    first = jnp.concatenate(
        [add([got_y2[i] for i in range(NZ)]), add([got_z2[i] for i in range(NY)])], axis=1
    ) * (1.0 / (NY * NZ)) + sr[...]
    middle, rest = compress(first)

    low = lax.broadcasted_iota(jnp.int32, (ROWS, 128), 1) < 64

    def fold(top, bottom):
        return (
            jnp.where(low, top, pltpu.roll(bottom, 64, axis=1)),
            jnp.where(low, pltpu.roll(top, 64, axis=1), bottom),
        )

    middle = middle.astype(F32)
    for k in range(NX):
        group = middle[:, 128 * k : 128 * k + 128]
        even, odd = fold(group[:16], group[16:])
        mid[2 * k] = even.astype(BF16)
        mid[2 * k + 1] = odd.astype(BF16)
    c_copies = []
    for dx in (2, 1, 3, 0):
        for dc in range(NC):
            if dx or dc:
                tx, tc = lax.rem(x + dx, NX), lax.rem(c + dc, NC)
                c_copies.append(
                    remote(mid.at[2 * tx + tc], got_c.at[2 * x + c], (m_s, m_r), 2 * dx + dc, (tx, y, z, tc))
                )
    got_c[2 * x + c] = mid[2 * x + c]
    rn[...] = rest
    keep(rn, rn_h)
    side = jnp.concatenate([sc[0:16, :], sc[16:32, :]], axis=1)
    for copy in c_copies:
        copy.wait_recv()
    second = add([got_c[i] for i in range(NX * NC)]) * (1.0 / (NX * NC)) + side
    final, rest = compress(second)

    fin[...] = final
    f_copies = [
        remote(fin, gat.at[c, y, x, z], (f_s, f_r), d, (x, y, lax.rem(z + d, NZ), c)) for d in far_first
    ]
    gat[c, y, x, z] = final
    loads[11].wait()
    for i in range(4):
        rows = pl.ds(256 * i, 256)
        ig[rows, :] = lax.dot_general(
            cot[rows, :], w[...], (((1,), (1,)), ((), ())), preferred_element_type=F32
        ).astype(BF16)
    keep(ig, ig_h)
    cn[0:16, :] = rest[:, 0:64]
    cn[16:32, :] = pltpu.roll(rest, 64, axis=1)[:, 0:64]
    keep(cn, cn_h)
    nearest = sorted(
        [(dx, dy) for dx in range(NX) for dy in range(NY)],
        key=lambda d: min(d[0], NX - d[0]) + min(d[1], NY - d[1]),
    )
    p_copies, t_copies = {}, {}
    mine = z // 4

    def part_of(near):
        return pl.ds(4 * mine if near else 4 - 4 * mine, 4)

    def to_plane(near):
        block = gat.at[c, y, x, part_of(near)]
        for dx, dy in nearest[:0:-1]:
            there = (lax.rem(x + dx, NX), lax.rem(y + dy, NY), z, c)
            p_copies[near, dx, dy] = remote(block, block, (p_s, p_r), (near, dx, dy), there)

    def to_sibling(near, dx, dy):
        if dx or dy:
            p_copies[near, dx, dy].wait_recv()
        sx, sy = lax.rem(x - dx + NX, NX), lax.rem(y - dy + NY, NY)
        block = gat.at[c, sy, sx, part_of(near)]
        t_copies[near, dx, dy] = remote(block, block, (t_s, t_r), (near, dx, dy), (x, y, z, 1 - c))

    def unpack(near, dx, dy):
        sx, sy = lax.rem(x - dx + NX, NX), lax.rem(y - dy + NY, NY)
        t_copies[near, dx, dy].wait_recv()
        for i in range(4):
            base = mine if near else 1 - mine
            sz = 4 * base + i
            halves = fold(gat[0, sy, sx, sz].astype(F32), gat[1, sy, sx, sz].astype(F32))
            rows = pl.ds(pl.multiple_of(sy * 64 + base * 32 + i // 2 * 16, 16), 16)
            for h in range(2):
                pieces[h, dx, rows, pl.ds(i % 2 * 128, 128)] = halves[h].astype(BF16)
        if dy == 2 and not near:
            for h in range(2):
                total = jnp.dot(interleave[...], pieces[h, dx], preferred_element_type=F32)
                for side in range(2):
                    avg[4 * side + sx, pl.ds(256 * h, 256), :] = total[:, 128 * side : 128 * side + 128]
            keep(avg.at[sx], avg_h.at[sx])
            keep(avg.at[4 + sx], avg_h.at[4 + sx])

    def piece_from(at):
        d = lax.rem(z - at + NZ, NZ)
        pltpu.make_async_remote_copy(
            src_ref=fin, dst_ref=gat.at[c, y, x, 0], send_sem=f_s.at[d], recv_sem=f_r.at[d],
            device_id=device(x, y, lax.rem(z + d, NZ), c), device_id_type=MESH,
        ).wait_recv()

    for i in range(1, 4):
        piece_from(4 * mine + lax.rem(z + i, 4))
    to_plane(1)
    for i in range(4):
        piece_from(4 - 4 * mine + i)
    to_plane(0)
    for at in nearest:
        to_sibling(1, *at)
    for at in nearest:
        to_sibling(0, *at)
        unpack(1, *at)
    for at in nearest:
        unpack(0, *at)

    sent = list(y_copies.values()) + z_copies + y2_copies + z2_copies + c_copies + f_copies
    for copy in sent + list(p_copies.values()) + list(t_copies.values()):
        copy.wait_send()
    for copy in outs:
        copy.wait()


def finish(avg, wn, ig, rn, cn, avg_out, wn_out, ig_out, rn_out, cn_out, sem):
    moves = [(ig, ig_out), (rn, rn_out.at[0, 0]), (cn, cn_out.at[0, 0])]
    moves += [(wn.at[q], wn_out.at[0, 0, :, pl.ds(1024 * q, 1024)]) for q in range(ROWS)]
    moves += [(avg.at[k], avg_out.at[:, pl.ds(128 * k, 128)]) for k in range(8)]
    copies = [pltpu.make_async_copy(src, dst, sem.at[i]) for i, (src, dst) in enumerate(moves)]
    for copy in copies:
        copy.start()
    for copy in copies:
        copy.wait()


def local(context, cotangent, out_weight, momentum, worker_error, server_rows, server_cols):
    anywhere = pl.BlockSpec(memory_space=pl.ANY)
    dma = pltpu.SemaphoreType.DMA
    args = (context, cotangent, out_weight, momentum, worker_error, server_rows, server_cols)
    held = pl.pallas_call(
        fused,
        out_shape=(
            pltpu.VMEM((8, 512, 128), F32),
            pltpu.VMEM((ROWS, LANES, 1024), F32),
            pltpu.VMEM((1024, 512), BF16),
            pltpu.VMEM((LANES, BLOCK), F32),
            pltpu.VMEM((LANES, 64), F32),
        ),
        in_specs=[anywhere] * 7,
        out_specs=[anywhere] * 5,
        scratch_shapes=[
            pltpu.VMEM((1024, 512), BF16),
            pltpu.VMEM((1024, 1024), BF16),
            pltpu.VMEM((512, 1024), BF16),
            pltpu.VMEM((8, 512, 128), F32),
            pltpu.VMEM((LANES, WIDTH), F32),
            pltpu.VMEM((LANES, BLOCK), F32),
            pltpu.VMEM((LANES, 64), F32),
            pltpu.VMEM((512, 1024), BF16),
            pltpu.VMEM((8, 512, 128), F32),
            pltpu.VMEM((8, 512, 128), F32),
            pltpu.VMEM((ROWS, LANES, 1024), F32),
            pltpu.VMEM((1024, 512), BF16),
            pltpu.VMEM((LANES, BLOCK), F32),
            pltpu.VMEM((LANES, 64), F32),
            pltpu.VMEM((NY, NZ, LANES, YC), BF16),
            pltpu.VMEM((NY, NZ, LANES, YC), BF16),
            pltpu.VMEM((NZ, NY, LANES, ZC), BF16),
            pltpu.VMEM((NZ, NY, LANES, ZC), BF16),
            pltpu.VMEM((NZ, LANES, YC), BF16),
            pltpu.VMEM((NZ, LANES, YC), BF16),
            pltpu.VMEM((NY, LANES, ZC), BF16),
            pltpu.VMEM((NY, LANES, ZC), BF16),
            pltpu.VMEM((NX * NC, 16, 128), BF16),
            pltpu.VMEM((NX * NC, 16, 128), BF16),
            pltpu.VMEM((16, 128), BF16),
            pltpu.VMEM((NC, NY, NX, NZ, 16, 128), BF16),
            pltpu.VMEM((256, 256), BF16),
            pltpu.VMEM((2, NX, 256, 256), BF16),
            dma((14,)), dma((12,)),
            dma((4, NY)), dma((4, NY)), dma((NZ,)), dma((NZ,)), dma((NZ,)), dma((NZ,)), dma((NY,)), dma((NY,)),
            dma((NX * NC,)), dma((NX * NC,)), dma((NZ,)), dma((NZ,)),
            dma((2, NX, NY)), dma((2, NX, NY)), dma((2, NX, NY)), dma((2, NX, NY)),
        ],
        compiler_params=pltpu.CompilerParams(
            collective_id=0, has_side_effects=True, vmem_limit_bytes=44 << 20
        ),
        cost_estimate=pl.CostEstimate(flops=2 << 30, bytes_accessed=13 << 20, transcendentals=1 << 19),
        name="fused",
    )(*[pltpu.with_memory_space_constraint(arg, pltpu.HBM) for arg in args])
    return pl.pallas_call(
        finish,
        out_shape=(
            jax.ShapeDtypeStruct((512, 1024), F32),
            jax.ShapeDtypeStruct((1, 1, LANES, WIDTH), F32),
            jax.ShapeDtypeStruct((1024, 512), BF16),
            jax.ShapeDtypeStruct((1, 1, LANES, BLOCK), F32),
            jax.ShapeDtypeStruct((1, 1, LANES, 64), F32),
        ),
        in_specs=[anywhere] * 5,
        out_specs=[anywhere] * 5,
        scratch_shapes=[dma((27,))],
        compiler_params=pltpu.CompilerParams(vmem_limit_bytes=16 << 20),
        cost_estimate=pl.CostEstimate(flops=0, bytes_accessed=5 << 20, transcendentals=0),
        name="finish",
    )(*held)


def solution(mesh):
    state = P("row", "col", None, None)
    tokens = P(("row", "col"), None)

    def body(*args):
        avg, wn, ig, rn, cn = local(*args)
        return ig, avg, wn, rn, cn

    return jax.shard_map(
        body,
        mesh=mesh,
        in_specs=(tokens, tokens, P(), P(), state, state, state),
        out_specs=(tokens, P(), state, state, state),
        check_vma=False,
    )
```

```python
import functools

import jax
import jax.numpy as jnp
from jax import lax
from jax.experimental import pallas as pl
from jax.experimental.pallas import tpu as pltpu
from jax.sharding import PartitionSpec as P

MESH = pl.DeviceIdType.MESH
F32, BF16 = jnp.float32, jnp.bfloat16

NX, NY, NZ, NC = 4, 4, 8, 2
LANES, WIDTH = 32, 16384
BLOCK = 512
YC = 384
ZC = BLOCK - YC
ROWS = 16


def place():
    row, col = lax.axis_index("row"), lax.axis_index("col")
    return col // NC, row // NZ, lax.rem(row, NZ), lax.rem(col, NC)


def device(x, y, z, c):
    return (y * NZ + z, x * NC + c)


def scale_of(total, count):
    return jnp.sqrt(total / count + 1e-06)


def total_of(values):
    return jnp.sum(jnp.sum(values, axis=0, keepdims=True), axis=1, keepdims=True)


def soft(values, scale, slope):
    return (scale * jnp.tanh(values * slope)).astype(BF16)


def compress(values):
    scale = scale_of(total_of(values * values), values.size)
    packed = soft(values, scale, 3.0 / scale)
    return packed, values - packed.astype(F32)


def partners():
    found = [(0, d, 0, 0) for d in range(1, NY)]
    found += [(0, 0, d, 0) for d in range(1, NZ)]
    found += [(dx, 0, 0, dc) for dx in range(NX) for dc in range(NC) if dx or dc]
    found += [(dx, dy, 0, 0) for dx in range(1, NX) for dy in range(1, NY)]
    return found


def fused(
    ctx_h, cot_h, w_h, mom_h, we_h, sr_h, sc_h,
    avg_h, wn_h, ig_h, rn_h, cn_h,
    ctx, cot, w, mom, we, sr, sc, ctx_t, grad, avg, vals, ig, rn, cn,
    send_y, got_y, send_z, got_z, part_y, got_y2, part_z, got_z2, mid, got_c, fin, gat, interleave, pieces,
    in_sem, out_sem, y_s, y_r, z_s, z_r, y2_s, y2_r, z2_s, z2_r, m_s, m_r, f_s, f_r, p_s, p_r, t_s, t_r,
):
    x, y, z, c = place()

    loads = [
        pltpu.make_async_copy(src, dst, in_sem.at[i])
        for i, (src, dst) in enumerate(
            [(ctx_h, ctx), (cot_h.at[:, pl.ds(0, 512)], cot.at[:, pl.ds(0, 512)]), (we_h.at[0, 0], we)]
            + [(mom_h.at[:, pl.ds(128 * k, 128)], mom.at[k]) for k in range(8)]
            + [(w_h, w), (sr_h.at[0, 0], sr), (sc_h.at[0, 0], sc), (cot_h.at[:, pl.ds(512, 512)], cot.at[:, pl.ds(512, 512)])]
        )
    ]
    for load in loads[:2] + loads[14:]:
        load.start()

    barrier = pltpu.get_barrier_semaphore()
    known = partners()
    for dx, dy, dz, dc in known:
        there = device(lax.rem(x + dx, NX), lax.rem(y + dy, NY), lax.rem(z + dz, NZ), lax.rem(c + dc, NC))
        pl.semaphore_signal(barrier, inc=1, device_id=there, device_id_type=MESH)

    for load in loads[2:14]:
        load.start()

    a = lax.broadcasted_iota(jnp.int32, (256, 256), 0)
    b = lax.broadcasted_iota(jnp.int32, (256, 256), 1)
    interleave[...] = jnp.where(b == lax.rem(a, ROWS) * ROWS + a // ROWS, 1.0, 0.0).astype(BF16)

    loads[0].wait()
    ctx_t[...] = ctx[...].T
    loads[1].wait()

    for n in range(4):
        if n == 2:
            loads[14].wait()
        product = jnp.dot(ctx_t[...], cot[:, 256 * n : 256 * n + 256], preferred_element_type=F32)
        grad[2 * n] = product[:, :128]
        grad[2 * n + 1] = product[:, 128:]

    total = jnp.zeros((8, 128), F32)
    loads[2].wait()
    for k in range(8):
        loads[3 + k].wait()
        for q in range(ROWS):
            rows = pl.ds(q, LANES, stride=ROWS)
            v = 0.9 * mom[k, rows, :] + 0.1 * grad[k, rows, :] + we[:, 1024 * q + 128 * k : 1024 * q + 128 * k + 128]
            vals[q, :, 128 * k : 128 * k + 128] = v
            v = v * v
            total = total + ((v[0:8] + v[8:16]) + (v[16:24] + v[24:32]))
    scale = scale_of(total_of(total), LANES * WIDTH)
    slope = 3.0 / scale

    pl.semaphore_wait(barrier, len(known))

    def remote(src, dst, sems, at, to):
        copy = pltpu.make_async_remote_copy(
            src_ref=src, dst_ref=dst, send_sem=sems[0].at[at], recv_sem=sems[1].at[at],
            device_id=device(*to), device_id_type=MESH,
        )
        copy.start()
        return copy

    outs = []

    def keep(src, dst):
        copy = pltpu.make_async_copy(src, dst, out_sem.at[len(outs)])
        copy.start()
        outs.append(copy)

    def add(parts):
        total = parts[0].astype(F32)
        for one in parts[1:]:
            total = total + one.astype(F32)
        return total

    order = (2, 1, 3, 0)
    y_copies, z_copies = {}, []

    def along_z(to):
        d = lax.rem(to - z + NZ, NZ)
        z_copies.append(remote(send_z.at[to], got_z.at[z], (z_s, z_r), d, (x, y, to, c)))

    for e in order:
        k = lax.rem(z // 2 + e, NZ // 2)
        for d in order:
            to = lax.rem(y + d, NY)
            q = to * 4 + k
            for half in range(2):
                cols = pl.ds(half * BLOCK, BLOCK)
                v = vals[q, :, cols]
                p = soft(v, scale, slope)
                if d:
                    send_y[to, 2 * k + half] = p[:, :YC]
                else:
                    got_y[y, 2 * k + half] = p[:, :YC]
                send_z[2 * k + half, to] = p[:, YC:]
                vals[q, :, cols] = v - p.astype(F32)
            if d:
                pair = pl.ds(2 * k, 2)
                y_copies[e, d] = remote(
                    send_y.at[to, pair], got_y.at[y, pair], (y_s, y_r), (e, d), (x, to, z, c)
                )
        if e:
            along_z(2 * k)
            along_z(2 * k + 1)
    other = z + 1 - 2 * lax.rem(z, 2)
    along_z(other)
    got_z[z] = send_z[z]
    keep(vals, wn_h)

    y2_copies, z2_copies = [], []

    def sum_y(at):
        return add([got_y[i, at] for i in range(NY)]).astype(BF16)

    def send_part(to):
        part_y[to] = sum_y(to)
        d = lax.rem(to - z + NZ, NZ)
        y2_copies.append(remote(part_y.at[to], got_y2.at[z], (y2_s, y2_r), d, (x, y, to, c)))

    for e in (2, 1, 3):
        for d in (2, 1, 3):
            y_copies[e, d].wait_recv()
        k = lax.rem(z // 2 + e, NZ // 2)
        send_part(2 * k)
        send_part(2 * k + 1)

    far_first = (4, 3, 5, 2, 6, 1, 7)

    def from_z(sems, d, block):
        pltpu.make_async_remote_copy(
            src_ref=block, dst_ref=block, send_sem=sems[0].at[d], recv_sem=sems[1].at[d],
            device_id=device(x, y, lax.rem(z + d, NZ), c), device_id_type=MESH,
        ).wait_recv()

    for d in (2, 1, 3):
        y_copies[0, d].wait_recv()
    send_part(other)
    got_y2[z] = sum_y(z)
    for d in far_first:
        from_z((z_s, z_r), d, got_z.at[0])
    for d in order:
        to = lax.rem(y + d, NY)
        total = add([got_z[i, to] for i in range(NZ)]).astype(BF16)
        if d:
            part_z[to] = total
            z2_copies.append(remote(part_z.at[to], got_z2.at[y], (z2_s, z2_r), d, (x, to, z, c)))
        else:
            got_z2[y] = total

    loads[12].wait()
    loads[13].wait()
    for copy in z2_copies:
        copy.wait_recv()
    for d in far_first:
        from_z((y2_s, y2_r), d, got_y2.at[0])
    first = jnp.concatenate(
        [add([got_y2[i] for i in range(NZ)]), add([got_z2[i] for i in range(NY)])], axis=1
    ) * (1.0 / (NY * NZ)) + sr[...]
    low = lax.broadcasted_iota(jnp.int32, (ROWS, 128), 1) < 64

    def fold(top, bottom):
        return (
            jnp.where(low, top, pltpu.roll(bottom, 64, axis=1)),
            jnp.where(low, pltpu.roll(top, 64, axis=1), bottom),
        )

    folded = [fold(first[:16, 128 * k : 128 * k + 128], first[16:, 128 * k : 128 * k + 128]) for k in range(NX)]
    scale = scale_of(total_of(first * first), LANES * BLOCK)
    slope = 3.0 / scale
    for k in range(NX):
        for h in range(NC):
            mid[2 * k + h] = soft(folded[k][h], scale, slope)
    c_copies = []
    for dx in (2, 1, 3, 0):
        for dc in range(NC):
            if dx or dc:
                tx, tc = lax.rem(x + dx, NX), lax.rem(c + dc, NC)
                c_copies.append(
                    remote(mid.at[2 * tx + tc], got_c.at[2 * x + c], (m_s, m_r), 2 * dx + dc, (tx, y, z, tc))
                )
    got_c[2 * x + c] = mid[2 * x + c]
    rn[...] = first - soft(first, scale, slope).astype(F32)
    keep(rn, rn_h)
    side = jnp.concatenate([sc[0:16, :], sc[16:32, :]], axis=1)
    for copy in c_copies:
        copy.wait_recv()
    second = add([got_c[i] for i in range(NX * NC)]) * (1.0 / (NX * NC)) + side
    final, rest = compress(second)

    fin[...] = final
    f_copies = [
        remote(fin, gat.at[c, y, x, z], (f_s, f_r), d, (x, y, lax.rem(z + d, NZ), c)) for d in far_first
    ]
    gat[c, y, x, z] = final
    loads[11].wait()
    for i in range(4):
        rows = pl.ds(256 * i, 256)
        ig[rows, :] = lax.dot_general(
            cot[rows, :], w[...], (((1,), (1,)), ((), ())), preferred_element_type=F32
        ).astype(BF16)
    keep(ig, ig_h)
    cn[0:16, :] = rest[:, 0:64]
    cn[16:32, :] = pltpu.roll(rest, 64, axis=1)[:, 0:64]
    keep(cn, cn_h)
    nearest = sorted(
        [(dx, dy) for dx in range(NX) for dy in range(NY)],
        key=lambda d: min(d[0], NX - d[0]) + min(d[1], NY - d[1]),
    )
    p_copies, t_copies = {}, {}
    mine = z // 4

    def part_of(near):
        return pl.ds(4 * mine if near else 4 - 4 * mine, 4)

    def to_plane(near):
        block = gat.at[c, y, x, part_of(near)]
        for dx, dy in nearest[:0:-1]:
            there = (lax.rem(x + dx, NX), lax.rem(y + dy, NY), z, c)
            p_copies[near, dx, dy] = remote(block, block, (p_s, p_r), (near, dx, dy), there)

    def to_sibling(near, dx, dy):
        if dx or dy:
            p_copies[near, dx, dy].wait_recv()
        sx, sy = lax.rem(x - dx + NX, NX), lax.rem(y - dy + NY, NY)
        block = gat.at[c, sy, sx, part_of(near)]
        t_copies[near, dx, dy] = remote(block, block, (t_s, t_r), (near, dx, dy), (x, y, z, 1 - c))

    def unpack(near, dx, dy):
        sx, sy = lax.rem(x - dx + NX, NX), lax.rem(y - dy + NY, NY)
        t_copies[near, dx, dy].wait_recv()
        for i in range(4):
            base = mine if near else 1 - mine
            sz = 4 * base + i
            halves = fold(gat[0, sy, sx, sz].astype(F32), gat[1, sy, sx, sz].astype(F32))
            rows = pl.ds(pl.multiple_of(sy * 64 + base * 32 + i // 2 * 16, 16), 16)
            for h in range(2):
                pieces[h, dx, rows, pl.ds(i % 2 * 128, 128)] = halves[h].astype(BF16)
        if dy == 2 and not near:
            for h in range(2):
                total = jnp.dot(interleave[...], pieces[h, dx], preferred_element_type=F32)
                for side in range(2):
                    avg[4 * side + sx, pl.ds(256 * h, 256), :] = total[:, 128 * side : 128 * side + 128]
            keep(avg.at[sx], avg_h.at[sx])
            keep(avg.at[4 + sx], avg_h.at[4 + sx])

    def piece_from(at):
        d = lax.rem(z - at + NZ, NZ)
        pltpu.make_async_remote_copy(
            src_ref=fin, dst_ref=gat.at[c, y, x, 0], send_sem=f_s.at[d], recv_sem=f_r.at[d],
            device_id=device(x, y, lax.rem(z + d, NZ), c), device_id_type=MESH,
        ).wait_recv()

    for i in range(1, 4):
        piece_from(4 * mine + lax.rem(z + i, 4))
    to_plane(1)
    for i in range(4):
        piece_from(4 - 4 * mine + i)
    to_plane(0)
    for at in nearest:
        to_sibling(1, *at)
    for at in nearest:
        to_sibling(0, *at)
        unpack(1, *at)
    for at in nearest:
        unpack(0, *at)

    sent = list(y_copies.values()) + z_copies + y2_copies + z2_copies + c_copies + f_copies
    for copy in sent + list(p_copies.values()) + list(t_copies.values()):
        copy.wait_send()
    for copy in outs:
        copy.wait()


def finish(avg, wn, ig, rn, cn, avg_out, wn_out, ig_out, rn_out, cn_out, sem):
    moves = [(ig, ig_out), (rn, rn_out.at[0, 0]), (cn, cn_out.at[0, 0])]
    moves += [(wn.at[q], wn_out.at[0, 0, :, pl.ds(1024 * q, 1024)]) for q in range(ROWS)]
    moves += [(avg.at[k], avg_out.at[:, pl.ds(128 * k, 128)]) for k in range(8)]
    copies = [pltpu.make_async_copy(src, dst, sem.at[i]) for i, (src, dst) in enumerate(moves)]
    for copy in copies:
        copy.start()
    for copy in copies:
        copy.wait()


def local(context, cotangent, out_weight, momentum, worker_error, server_rows, server_cols):
    anywhere = pl.BlockSpec(memory_space=pl.ANY)
    dma = pltpu.SemaphoreType.DMA
    args = (context, cotangent, out_weight, momentum, worker_error, server_rows, server_cols)
    held = pl.pallas_call(
        fused,
        out_shape=(
            pltpu.VMEM((8, 512, 128), F32),
            pltpu.VMEM((ROWS, LANES, 1024), F32),
            pltpu.VMEM((1024, 512), BF16),
            pltpu.VMEM((LANES, BLOCK), F32),
            pltpu.VMEM((LANES, 64), F32),
        ),
        in_specs=[anywhere] * 7,
        out_specs=[anywhere] * 5,
        scratch_shapes=[
            pltpu.VMEM((1024, 512), BF16),
            pltpu.VMEM((1024, 1024), BF16),
            pltpu.VMEM((512, 1024), BF16),
            pltpu.VMEM((8, 512, 128), F32),
            pltpu.VMEM((LANES, WIDTH), F32),
            pltpu.VMEM((LANES, BLOCK), F32),
            pltpu.VMEM((LANES, 64), F32),
            pltpu.VMEM((512, 1024), BF16),
            pltpu.VMEM((8, 512, 128), F32),
            pltpu.VMEM((8, 512, 128), F32),
            pltpu.VMEM((ROWS, LANES, 1024), F32),
            pltpu.VMEM((1024, 512), BF16),
            pltpu.VMEM((LANES, BLOCK), F32),
            pltpu.VMEM((LANES, 64), F32),
            pltpu.VMEM((NY, NZ, LANES, YC), BF16),
            pltpu.VMEM((NY, NZ, LANES, YC), BF16),
            pltpu.VMEM((NZ, NY, LANES, ZC), BF16),
            pltpu.VMEM((NZ, NY, LANES, ZC), BF16),
            pltpu.VMEM((NZ, LANES, YC), BF16),
            pltpu.VMEM((NZ, LANES, YC), BF16),
            pltpu.VMEM((NY, LANES, ZC), BF16),
            pltpu.VMEM((NY, LANES, ZC), BF16),
            pltpu.VMEM((NX * NC, 16, 128), BF16),
            pltpu.VMEM((NX * NC, 16, 128), BF16),
            pltpu.VMEM((16, 128), BF16),
            pltpu.VMEM((NC, NY, NX, NZ, 16, 128), BF16),
            pltpu.VMEM((256, 256), BF16),
            pltpu.VMEM((2, NX, 256, 256), BF16),
            dma((15,)), dma((12,)),
            dma((4, NY)), dma((4, NY)), dma((NZ,)), dma((NZ,)), dma((NZ,)), dma((NZ,)), dma((NY,)), dma((NY,)),
            dma((NX * NC,)), dma((NX * NC,)), dma((NZ,)), dma((NZ,)),
            dma((2, NX, NY)), dma((2, NX, NY)), dma((2, NX, NY)), dma((2, NX, NY)),
        ],
        compiler_params=pltpu.CompilerParams(
            collective_id=0, has_side_effects=True, vmem_limit_bytes=44 << 20
        ),
        cost_estimate=pl.CostEstimate(flops=2 << 30, bytes_accessed=13 << 20, transcendentals=1 << 19),
        name="fused",
    )(*[pltpu.with_memory_space_constraint(arg, pltpu.HBM) for arg in args])
    return pl.pallas_call(
        finish,
        out_shape=(
            jax.ShapeDtypeStruct((512, 1024), F32),
            jax.ShapeDtypeStruct((1, 1, LANES, WIDTH), F32),
            jax.ShapeDtypeStruct((1024, 512), BF16),
            jax.ShapeDtypeStruct((1, 1, LANES, BLOCK), F32),
            jax.ShapeDtypeStruct((1, 1, LANES, 64), F32),
        ),
        in_specs=[anywhere] * 5,
        out_specs=[anywhere] * 5,
        scratch_shapes=[dma((27,))],
        compiler_params=pltpu.CompilerParams(vmem_limit_bytes=16 << 20),
        cost_estimate=pl.CostEstimate(flops=0, bytes_accessed=5 << 20, transcendentals=0),
        name="finish",
    )(*held)


def solution(mesh):
    state = P("row", "col", None, None)
    tokens = P(("row", "col"), None)

    def body(*args):
        avg, wn, ig, rn, cn = local(*args)
        return ig, avg, wn, rn, cn

    return jax.shard_map(
        body,
        mesh=mesh,
        in_specs=(tokens, tokens, P(), P(), state, state, state),
        out_specs=(tokens, P(), state, state, state),
        check_vma=False,
    )
```

```python
import functools

import jax
import jax.numpy as jnp
from jax import lax
from jax.experimental import pallas as pl
from jax.experimental.pallas import tpu as pltpu
from jax.sharding import PartitionSpec as P

MESH = pl.DeviceIdType.MESH
F32, BF16 = jnp.float32, jnp.bfloat16

NX, NY, NZ, NC = 4, 4, 8, 2
LANES, WIDTH = 32, 16384
BLOCK = 512
YC = 384
ZC = BLOCK - YC
ROWS = 16


def place():
    row, col = lax.axis_index("row"), lax.axis_index("col")
    return col // NC, row // NZ, lax.rem(row, NZ), lax.rem(col, NC)


def device(x, y, z, c):
    return (y * NZ + z, x * NC + c)


def scale_of(total, count):
    return jnp.sqrt(total / count + 1e-06)


def total_of(values):
    return jnp.sum(jnp.sum(values, axis=0, keepdims=True), axis=1, keepdims=True)


def soft(values, scale, slope):
    return (scale * jnp.tanh(values * slope)).astype(BF16)


def compress(values):
    scale = scale_of(total_of(values * values), values.size)
    packed = soft(values, scale, 3.0 / scale)
    return packed, values - packed.astype(F32)


def partners():
    found = [(0, d, 0, 0) for d in range(1, NY)]
    found += [(0, 0, d, 0) for d in range(1, NZ)]
    found += [(dx, 0, 0, dc) for dx in range(NX) for dc in range(NC) if dx or dc]
    found += [(dx, dy, 0, 0) for dx in range(1, NX) for dy in range(1, NY)]
    return found


def fused(
    ctx_h, cot_h, w_h, mom_h, we_h, sr_h, sc_h,
    avg_h, wn_h, ig_h, rn_h, cn_h,
    ctx, cot, w, mom, we, sr, sc, ctx_t, grad, avg, vals, ig, rn, cn,
    send_y, got_y, send_z, got_z, part_y, got_y2, part_z, got_z2, mid, got_c, fin, gat,
    in_sem, out_sem, y_s, y_r, z_s, z_r, y2_s, y2_r, z2_s, z2_r, m_s, m_r, f_s, f_r, p_s, p_r, t_s, t_r,
):
    x, y, z, c = place()

    loads = [
        pltpu.make_async_copy(src, dst, in_sem.at[i])
        for i, (src, dst) in enumerate(
            [(ctx_h, ctx), (cot_h.at[:, pl.ds(0, 512)], cot.at[:, pl.ds(0, 512)]), (we_h.at[0, 0], we)]
            + [(mom_h.at[:, pl.ds(128 * k, 128)], mom.at[k]) for k in range(8)]
            + [(w_h, w), (sr_h.at[0, 0], sr), (sc_h.at[0, 0], sc), (cot_h.at[:, pl.ds(512, 512)], cot.at[:, pl.ds(512, 512)])]
        )
    ]
    for load in loads[:2] + loads[14:]:
        load.start()

    barrier = pltpu.get_barrier_semaphore()
    known = partners()
    for dx, dy, dz, dc in known:
        there = device(lax.rem(x + dx, NX), lax.rem(y + dy, NY), lax.rem(z + dz, NZ), lax.rem(c + dc, NC))
        pl.semaphore_signal(barrier, inc=1, device_id=there, device_id_type=MESH)

    for load in loads[3:11] + loads[2:3] + loads[11:14]:
        load.start()

    loads[0].wait()
    ctx_t[...] = ctx[...].T
    loads[1].wait()

    for n in range(4):
        if n == 2:
            loads[14].wait()
        product = jnp.dot(ctx_t[...], cot[:, 256 * n : 256 * n + 256], preferred_element_type=F32)
        grad[2 * n] = product[:, :128]
        grad[2 * n + 1] = product[:, 128:]

    for k in range(8):
        loads[3 + k].wait()
        grad[k] = 0.9 * mom[k] + 0.1 * grad[k]
    total = jnp.zeros((8, 128), F32)
    loads[2].wait()
    for q in range(ROWS):
        for k in range(8):
            v = grad[k, pl.ds(q, LANES, stride=ROWS), :] + we[:, 1024 * q + 128 * k : 1024 * q + 128 * k + 128]
            vals[q, :, 128 * k : 128 * k + 128] = v
            v = v * v
            total = total + ((v[0:8] + v[8:16]) + (v[16:24] + v[24:32]))
    scale = scale_of(total_of(total), LANES * WIDTH)
    slope = 3.0 / scale

    pl.semaphore_wait(barrier, len(known))

    def remote(src, dst, sems, at, to):
        copy = pltpu.make_async_remote_copy(
            src_ref=src, dst_ref=dst, send_sem=sems[0].at[at], recv_sem=sems[1].at[at],
            device_id=device(*to), device_id_type=MESH,
        )
        copy.start()
        return copy

    outs = []

    def keep(src, dst):
        copy = pltpu.make_async_copy(src, dst, out_sem.at[len(outs)])
        copy.start()
        outs.append(copy)

    def finished(copies):
        for copy in copies:
            copy.wait_send()

    def add(parts):
        total = parts[0].astype(F32)
        for one in parts[1:]:
            total = total + one.astype(F32)
        return total

    order = (2, 1, 3, 0)
    y_copies, z_copies = {}, []

    def along_z(to):
        d = lax.rem(to - z + NZ, NZ)
        z_copies.append(remote(send_z.at[to], got_z.at[z], (z_s, z_r), d, (x, y, to, c)))

    for e in order:
        k = lax.rem(z // 2 + e, NZ // 2)
        for d in order:
            to = lax.rem(y + d, NY)
            q = to * 4 + k
            for half in range(2):
                cols = pl.ds(half * BLOCK, BLOCK)
                v = vals[q, :, cols]
                p = soft(v, scale, slope)
                if d:
                    send_y[to, 2 * k + half] = p[:, :YC]
                else:
                    got_y[y, 2 * k + half] = p[:, :YC]
                send_z[2 * k + half, to] = p[:, YC:]
                vals[q, :, cols] = v - p.astype(F32)
            if d:
                pair = pl.ds(2 * k, 2)
                y_copies[e, d] = remote(
                    send_y.at[to, pair], got_y.at[y, pair], (y_s, y_r), (e, d), (x, to, z, c)
                )
        if e:
            along_z(2 * k)
            along_z(2 * k + 1)
    other = z + 1 - 2 * lax.rem(z, 2)
    along_z(other)
    got_z[z] = send_z[z]
    keep(vals, wn_h)

    y2_copies, z2_copies = [], []

    def sum_y(at):
        return add([got_y[i, at] for i in range(NY)]).astype(BF16)

    def send_part(to):
        part_y[to] = sum_y(to)
        d = lax.rem(to - z + NZ, NZ)
        y2_copies.append(remote(part_y.at[to], got_y2.at[z], (y2_s, y2_r), d, (x, y, to, c)))

    for e in (2, 1, 3):
        for d in (2, 1, 3):
            y_copies[e, d].wait_recv()
        k = lax.rem(z // 2 + e, NZ // 2)
        send_part(2 * k)
        send_part(2 * k + 1)

    far_first = (4, 3, 5, 2, 6, 1, 7)

    def from_z(sems, d, block):
        pltpu.make_async_remote_copy(
            src_ref=block, dst_ref=block, send_sem=sems[0].at[d], recv_sem=sems[1].at[d],
            device_id=device(x, y, lax.rem(z + d, NZ), c), device_id_type=MESH,
        ).wait_recv()

    for d in (2, 1, 3):
        y_copies[0, d].wait_recv()
    send_part(other)
    got_y2[z] = sum_y(z)
    for d in far_first:
        from_z((z_s, z_r), d, got_z.at[0])
    for d in order:
        to = lax.rem(y + d, NY)
        total = add([got_z[i, to] for i in range(NZ)]).astype(BF16)
        if d:
            part_z[to] = total
            z2_copies.append(remote(part_z.at[to], got_z2.at[y], (z2_s, z2_r), d, (x, to, z, c)))
        else:
            got_z2[y] = total

    finished(list(y_copies.values()) + z_copies)
    loads[12].wait()
    loads[13].wait()
    for copy in z2_copies:
        copy.wait_recv()
    for d in far_first:
        from_z((y2_s, y2_r), d, got_y2.at[0])
    first = jnp.concatenate(
        [add([got_y2[i] for i in range(NZ)]), add([got_z2[i] for i in range(NY)])], axis=1
    ) * (1.0 / (NY * NZ)) + sr[...]
    def low_of(half):
        return lax.broadcasted_iota(jnp.int32, half.shape, 1) < 64

    def fold(top, bottom):
        return (
            jnp.where(low_of(top), top, pltpu.roll(bottom, 64, axis=1)),
            jnp.where(low_of(top), pltpu.roll(top, 64, axis=1), bottom),
        )

    folded = [fold(first[:16, 128 * k : 128 * k + 128], first[16:, 128 * k : 128 * k + 128]) for k in range(NX)]
    scale = scale_of(total_of(first * first), LANES * BLOCK)
    slope = 3.0 / scale
    for k in range(NX):
        for h in range(NC):
            mid[2 * k + h] = soft(folded[k][h], scale, slope)
    c_copies = []
    for dx in (2, 1, 3, 0):
        for dc in range(NC):
            if dx or dc:
                tx, tc = lax.rem(x + dx, NX), lax.rem(c + dc, NC)
                c_copies.append(
                    remote(mid.at[2 * tx + tc], got_c.at[2 * x + c], (m_s, m_r), 2 * dx + dc, (tx, y, z, tc))
                )
    got_c[2 * x + c] = mid[2 * x + c]
    rn[...] = first - soft(first, scale, slope).astype(F32)
    keep(rn, rn_h)
    side = jnp.concatenate([sc[0:16, :], sc[16:32, :]], axis=1)
    finished(y2_copies + z2_copies)
    for copy in c_copies:
        copy.wait_recv()
    second = add([got_c[i] for i in range(NX * NC)]) * (1.0 / (NX * NC)) + side
    final, rest = compress(second)

    fin[...] = final
    f_copies = [
        remote(fin, gat.at[c, x, lax.rem(z, 2), y, z // 2], (f_s, f_r), d, (x, y, lax.rem(z + d, NZ), c)) for d in far_first
    ]
    gat[c, x, lax.rem(z, 2), y, z // 2] = final
    loads[11].wait()
    for i in range(4):
        rows = pl.ds(256 * i, 256)
        ig[rows, :] = lax.dot_general(
            cot[rows, :], w[...], (((1,), (1,)), ((), ())), preferred_element_type=F32
        ).astype(BF16)
    keep(ig, ig_h)
    cn[0:16, :] = rest[:, 0:64]
    cn[16:32, :] = pltpu.roll(rest, 64, axis=1)[:, 0:64]
    keep(cn, cn_h)
    nearest = sorted(
        [(dx, dy) for dx in range(NX) for dy in range(NY)],
        key=lambda d: min(d[0], NX - d[0]) + min(d[1], NY - d[1]),
    )
    p_copies, t_copies = {}, {}
    mine = z // 4

    def part_of(near):
        return pl.ds(2 * mine if near else 2 - 2 * mine, 2)

    def to_plane(near):
        block = gat.at[c, x, :, y, part_of(near)]
        for dx, dy in nearest[:0:-1]:
            there = (lax.rem(x + dx, NX), lax.rem(y + dy, NY), z, c)
            p_copies[near, dx, dy] = remote(block, block, (p_s, p_r), (near, dx, dy), there)

    def to_sibling(near, dx, dy):
        if dx or dy:
            p_copies[near, dx, dy].wait_recv()
        sx, sy = lax.rem(x - dx + NX, NX), lax.rem(y - dy + NY, NY)
        block = gat.at[c, sx, :, sy, part_of(near)]
        t_copies[near, dx, dy] = remote(block, block, (t_s, t_r), (near, dx, dy), (x, y, z, 1 - c))

    def unpack(dx):
        sx = lax.rem(x - dx + NX, NX)
        for h in range(2):
            for sy in range(NY):
                for i in range(NZ // 2):
                    halves = fold(gat[0, sx, h, sy, i], gat[1, sx, h, sy, i])
                    for side in range(2):
                        rows = pl.ds(256 * side + 4 * sy + i, 16, stride=ROWS)
                        avg[4 * h + sx, rows, :] = halves[side].astype(F32)
            keep(avg.at[4 * h + sx], avg_h.at[4 * h + sx])

    def piece_from(at):
        d = lax.rem(z - at + NZ, NZ)
        pltpu.make_async_remote_copy(
            src_ref=fin, dst_ref=gat.at[c, x, 0, y, 0], send_sem=f_s.at[d], recv_sem=f_r.at[d],
            device_id=device(x, y, lax.rem(z + d, NZ), c), device_id_type=MESH,
        ).wait_recv()

    finished(c_copies)
    for i in range(1, 4):
        piece_from(4 * mine + lax.rem(z + i, 4))
    to_plane(1)
    for i in range(4):
        piece_from(4 - 4 * mine + i)
    to_plane(0)
    finished(f_copies)
    for copy in outs[:4]:
        copy.wait()
    for at in nearest:
        to_sibling(1, *at)
    for at in nearest:
        to_sibling(0, *at)
    finished([p_copies[1, dx, dy] for dx, dy in nearest[1:]])
    for dx in (0, 1, 3, 2):
        for near in (1, 0):
            for dy in range(NY):
                t_copies[near, dx, dy].wait_recv()
        unpack(dx)
    finished([p_copies[0, dx, dy] for dx, dy in nearest[1:]] + [t_copies[1, dx, dy] for dx, dy in nearest])
    finished([t_copies[0, dx, dy] for dx, dy in nearest])
    for copy in outs[4:]:
        copy.wait()


def finish(avg, wn, ig, rn, cn, avg_out, wn_out, ig_out, rn_out, cn_out, sem):
    moves = [(ig, ig_out), (rn, rn_out.at[0, 0]), (cn, cn_out.at[0, 0])]
    moves += [(wn.at[q], wn_out.at[0, 0, :, pl.ds(1024 * q, 1024)]) for q in range(ROWS)]
    moves += [(avg.at[k], avg_out.at[:, pl.ds(128 * k, 128)]) for k in range(8)]
    copies = [pltpu.make_async_copy(src, dst, sem.at[i]) for i, (src, dst) in enumerate(moves)]
    for copy in copies:
        copy.start()
    for copy in copies:
        copy.wait()


def local(context, cotangent, out_weight, momentum, worker_error, server_rows, server_cols):
    anywhere = pl.BlockSpec(memory_space=pl.ANY)
    dma = pltpu.SemaphoreType.DMA
    args = (context, cotangent, out_weight, momentum, worker_error, server_rows, server_cols)
    held = pl.pallas_call(
        fused,
        out_shape=(
            pltpu.VMEM((8, 512, 128), F32),
            pltpu.VMEM((ROWS, LANES, 1024), F32),
            pltpu.VMEM((1024, 512), BF16),
            pltpu.VMEM((LANES, BLOCK), F32),
            pltpu.VMEM((LANES, 64), F32),
        ),
        in_specs=[anywhere] * 7,
        out_specs=[anywhere] * 5,
        scratch_shapes=[
            pltpu.VMEM((1024, 512), BF16),
            pltpu.VMEM((1024, 1024), BF16),
            pltpu.VMEM((512, 1024), BF16),
            pltpu.VMEM((8, 512, 128), F32),
            pltpu.VMEM((LANES, WIDTH), F32),
            pltpu.VMEM((LANES, BLOCK), F32),
            pltpu.VMEM((LANES, 64), F32),
            pltpu.VMEM((512, 1024), BF16),
            pltpu.VMEM((8, 512, 128), F32),
            pltpu.VMEM((8, 512, 128), F32),
            pltpu.VMEM((ROWS, LANES, 1024), F32),
            pltpu.VMEM((1024, 512), BF16),
            pltpu.VMEM((LANES, BLOCK), F32),
            pltpu.VMEM((LANES, 64), F32),
            pltpu.VMEM((NY, NZ, LANES, YC), BF16),
            pltpu.VMEM((NY, NZ, LANES, YC), BF16),
            pltpu.VMEM((NZ, NY, LANES, ZC), BF16),
            pltpu.VMEM((NZ, NY, LANES, ZC), BF16),
            pltpu.VMEM((NZ, LANES, YC), BF16),
            pltpu.VMEM((NZ, LANES, YC), BF16),
            pltpu.VMEM((NY, LANES, ZC), BF16),
            pltpu.VMEM((NY, LANES, ZC), BF16),
            pltpu.VMEM((NX * NC, 16, 128), BF16),
            pltpu.VMEM((NX * NC, 16, 128), BF16),
            pltpu.VMEM((16, 128), BF16),
            pltpu.VMEM((NC, NX, 2, NY, NZ // 2, 16, 128), BF16),
            dma((15,)), dma((12,)),
            dma((4, NY)), dma((4, NY)), dma((NZ,)), dma((NZ,)), dma((NZ,)), dma((NZ,)), dma((NY,)), dma((NY,)),
            dma((NX * NC,)), dma((NX * NC,)), dma((NZ,)), dma((NZ,)),
            dma((2, NX, NY)), dma((2, NX, NY)), dma((2, NX, NY)), dma((2, NX, NY)),
        ],
        compiler_params=pltpu.CompilerParams(
            collective_id=0, has_side_effects=True, vmem_limit_bytes=44 << 20
        ),
        cost_estimate=pl.CostEstimate(flops=2 << 30, bytes_accessed=13 << 20, transcendentals=1 << 19),
        name="fused",
    )(*[pltpu.with_memory_space_constraint(arg, pltpu.HBM) for arg in args])
    return pl.pallas_call(
        finish,
        out_shape=(
            jax.ShapeDtypeStruct((512, 1024), F32),
            jax.ShapeDtypeStruct((1, 1, LANES, WIDTH), F32),
            jax.ShapeDtypeStruct((1024, 512), BF16),
            jax.ShapeDtypeStruct((1, 1, LANES, BLOCK), F32),
            jax.ShapeDtypeStruct((1, 1, LANES, 64), F32),
        ),
        in_specs=[anywhere] * 5,
        out_specs=[anywhere] * 5,
        scratch_shapes=[dma((27,))],
        compiler_params=pltpu.CompilerParams(vmem_limit_bytes=16 << 20),
        cost_estimate=pl.CostEstimate(flops=0, bytes_accessed=5 << 20, transcendentals=0),
        name="finish",
    )(*held)


def solution(mesh):
    state = P("row", "col", None, None)
    tokens = P(("row", "col"), None)

    def body(*args):
        avg, wn, ig, rn, cn = local(*args)
        return ig, avg, wn, rn, cn

    return jax.shard_map(
        body,
        mesh=mesh,
        in_specs=(tokens, tokens, P(), P(), state, state, state),
        out_specs=(tokens, P(), state, state, state),
        check_vma=False,
    )
```

```python
import functools

import jax
import jax.numpy as jnp
from jax import lax
from jax.experimental import pallas as pl
from jax.experimental.pallas import tpu as pltpu
from jax.sharding import PartitionSpec as P

MESH = pl.DeviceIdType.MESH
F32, BF16 = jnp.float32, jnp.bfloat16

NX, NY, NZ, NC = 4, 4, 8, 2
LANES, WIDTH = 32, 16384
BLOCK = 512
YC = 384
ZC = BLOCK - YC
ROWS = 16


def place():
    row, col = lax.axis_index("row"), lax.axis_index("col")
    return col // NC, row // NZ, lax.rem(row, NZ), lax.rem(col, NC)


def device(x, y, z, c):
    return (y * NZ + z, x * NC + c)


def scale_of(total, count):
    return jnp.sqrt(total / count + 1e-06)


def total_of(values):
    return jnp.sum(jnp.sum(values, axis=0, keepdims=True), axis=1, keepdims=True)


def soft(values, scale, slope):
    return (scale * jnp.tanh(values * slope)).astype(BF16)


def compress(values):
    scale = scale_of(total_of(values * values), values.size)
    packed = soft(values, scale, 3.0 / scale)
    return packed, values - packed.astype(F32)


def partners():
    found = [(0, d, 0, 0) for d in range(1, NY)]
    found += [(0, 0, d, 0) for d in range(1, NZ)]
    found += [(dx, 0, 0, dc) for dx in range(NX) for dc in range(NC) if dx or dc]
    found += [(dx, dy, 0, 0) for dx in range(1, NX) for dy in range(1, NY)]
    return found


def fused(
    ctx_h, cot_h, w_h, mom_h, we_h, sr_h, sc_h,
    avg_h, wn_h, ig_h, rn_h, cn_h,
    ctx, cot, w, mom, we, sr, sc, ctx_t, grad, avg, vals, ig, rn, cn,
    send_y, got_y, send_z, got_z, part_y, got_y2, part_z, got_z2, mid, got_c, fin, gat,
    in_sem, out_sem, y_s, y_r, z_s, z_r, y2_s, y2_r, z2_s, z2_r, m_s, m_r, f_s, f_r, p_s, p_r, t_s, t_r,
):
    x, y, z, c = place()

    loads = [
        pltpu.make_async_copy(src, dst, in_sem.at[i])
        for i, (src, dst) in enumerate(
            [(ctx_h, ctx), (cot_h.at[:, pl.ds(0, 512)], cot.at[:, pl.ds(0, 512)]), (we_h.at[0, 0, :, pl.ds(0, 4096)], we.at[:, pl.ds(0, 4096)])]
            + [(mom_h.at[:, pl.ds(128 * k, 128)], mom.at[k]) for k in range(8)]
            + [(w_h, w), (sr_h.at[0, 0], sr), (sc_h.at[0, 0], sc), (cot_h.at[:, pl.ds(512, 512)], cot.at[:, pl.ds(512, 512)])]
            + [(we_h.at[0, 0, :, pl.ds(4096 * i, 4096)], we.at[:, pl.ds(4096 * i, 4096)]) for i in range(1, 4)]
        )
    ]
    for load in loads[:2] + loads[14:15]:
        load.start()

    barrier = pltpu.get_barrier_semaphore()
    known = partners()
    for dx, dy, dz, dc in known:
        there = device(lax.rem(x + dx, NX), lax.rem(y + dy, NY), lax.rem(z + dz, NZ), lax.rem(c + dc, NC))
        pl.semaphore_signal(barrier, inc=1, device_id=there, device_id_type=MESH)

    for load in loads[3:11] + loads[2:3] + loads[15:] + loads[11:14]:
        load.start()

    loads[0].wait()
    ctx_t[...] = ctx[...].T
    loads[1].wait()

    for n in range(4):
        if n == 2:
            loads[14].wait()
        product = jnp.dot(ctx_t[...], cot[:, 256 * n : 256 * n + 256], preferred_element_type=F32)
        grad[2 * n] = product[:, :128]
        grad[2 * n + 1] = product[:, 128:]

    for k in range(8):
        loads[3 + k].wait()
        grad[k] = 0.9 * mom[k] + 0.1 * grad[k]
    total = jnp.zeros((8, 128), F32)
    for q in range(ROWS):
        if q % 4 == 0:
            loads[14 + q // 4 if q else 2].wait()
        for k in range(8):
            v = grad[k, pl.ds(q, LANES, stride=ROWS), :] + we[:, 1024 * q + 128 * k : 1024 * q + 128 * k + 128]
            vals[q, :, 128 * k : 128 * k + 128] = v
            v = v * v
            total = total + ((v[0:8] + v[8:16]) + (v[16:24] + v[24:32]))
    scale = scale_of(total_of(total), LANES * WIDTH)
    slope = 3.0 / scale

    pl.semaphore_wait(barrier, len(known))

    def remote(src, dst, sems, at, to):
        copy = pltpu.make_async_remote_copy(
            src_ref=src, dst_ref=dst, send_sem=sems[0].at[at], recv_sem=sems[1].at[at],
            device_id=device(*to), device_id_type=MESH,
        )
        copy.start()
        return copy

    outs = []

    def keep(src, dst):
        copy = pltpu.make_async_copy(src, dst, out_sem.at[len(outs)])
        copy.start()
        outs.append(copy)

    def finished(copies):
        for copy in copies:
            copy.wait_send()

    def add(parts):
        total = parts[0].astype(F32)
        for one in parts[1:]:
            total = total + one.astype(F32)
        return total

    order = (2, 1, 3, 0)
    y_copies, z_copies = {}, []

    def along_z(to):
        d = lax.rem(to - z + NZ, NZ)
        z_copies.append(remote(send_z.at[to], got_z.at[z], (z_s, z_r), d, (x, y, to, c)))

    for e in order:
        k = lax.rem(z // 2 + e, NZ // 2)
        for d in order:
            to = lax.rem(y + d, NY)
            q = to * 4 + k
            for half in range(2):
                cols = pl.ds(half * BLOCK, BLOCK)
                v = vals[q, :, cols]
                p = soft(v, scale, slope)
                if d:
                    send_y[to, 2 * k + half] = p[:, :YC]
                else:
                    got_y[y, 2 * k + half] = p[:, :YC]
                send_z[2 * k + half, to] = p[:, YC:]
                vals[q, :, cols] = v - p.astype(F32)
            if d:
                pair = pl.ds(2 * k, 2)
                y_copies[e, d] = remote(
                    send_y.at[to, pair], got_y.at[y, pair], (y_s, y_r), (e, d), (x, to, z, c)
                )
        if e:
            along_z(2 * k)
            along_z(2 * k + 1)
    other = z + 1 - 2 * lax.rem(z, 2)
    along_z(other)
    got_z[z] = send_z[z]
    keep(vals, wn_h)

    y2_copies, z2_copies = [], []

    def sum_y(at):
        return add([got_y[i, at] for i in range(NY)]).astype(BF16)

    def send_part(to):
        part_y[to] = sum_y(to)
        d = lax.rem(to - z + NZ, NZ)
        y2_copies.append(remote(part_y.at[to], got_y2.at[z], (y2_s, y2_r), d, (x, y, to, c)))

    for e in (2, 1, 3):
        for d in (2, 1, 3):
            y_copies[e, d].wait_recv()
        k = lax.rem(z // 2 + e, NZ // 2)
        send_part(2 * k)
        send_part(2 * k + 1)

    far_first = (4, 3, 5, 2, 6, 1, 7)

    def from_z(sems, d, block):
        pltpu.make_async_remote_copy(
            src_ref=block, dst_ref=block, send_sem=sems[0].at[d], recv_sem=sems[1].at[d],
            device_id=device(x, y, lax.rem(z + d, NZ), c), device_id_type=MESH,
        ).wait_recv()

    for d in (2, 1, 3):
        y_copies[0, d].wait_recv()
    send_part(other)
    got_y2[z] = sum_y(z)
    for d in far_first:
        from_z((z_s, z_r), d, got_z.at[0])
    for d in order:
        to = lax.rem(y + d, NY)
        total = add([got_z[i, to] for i in range(NZ)]).astype(BF16)
        if d:
            part_z[to] = total
            z2_copies.append(remote(part_z.at[to], got_z2.at[y], (z2_s, z2_r), d, (x, to, z, c)))
        else:
            got_z2[y] = total

    finished(list(y_copies.values()) + z_copies)
    loads[12].wait()
    loads[13].wait()
    for copy in z2_copies:
        copy.wait_recv()
    for d in far_first:
        from_z((y2_s, y2_r), d, got_y2.at[0])
    first = jnp.concatenate(
        [add([got_y2[i] for i in range(NZ)]), add([got_z2[i] for i in range(NY)])], axis=1
    ) * (1.0 / (NY * NZ)) + sr[...]
    def low_of(half):
        return lax.broadcasted_iota(jnp.int32, half.shape, 1) < 64

    def fold(top, bottom):
        return (
            jnp.where(low_of(top), top, pltpu.roll(bottom, 64, axis=1)),
            jnp.where(low_of(top), pltpu.roll(top, 64, axis=1), bottom),
        )

    folded = [fold(first[:16, 128 * k : 128 * k + 128], first[16:, 128 * k : 128 * k + 128]) for k in range(NX)]
    scale = scale_of(total_of(first * first), LANES * BLOCK)
    slope = 3.0 / scale
    for k in range(NX):
        for h in range(NC):
            mid[2 * k + h] = soft(folded[k][h], scale, slope)
    c_copies = []
    for dx in (2, 1, 3, 0):
        for dc in range(NC):
            if dx or dc:
                tx, tc = lax.rem(x + dx, NX), lax.rem(c + dc, NC)
                c_copies.append(
                    remote(mid.at[2 * tx + tc], got_c.at[2 * x + c], (m_s, m_r), 2 * dx + dc, (tx, y, z, tc))
                )
    got_c[2 * x + c] = mid[2 * x + c]
    rn[...] = first - soft(first, scale, slope).astype(F32)
    keep(rn, rn_h)
    side = jnp.concatenate([sc[0:16, :], sc[16:32, :]], axis=1)
    finished(y2_copies + z2_copies)
    for copy in c_copies:
        copy.wait_recv()
    second = add([got_c[i] for i in range(NX * NC)]) * (1.0 / (NX * NC)) + side
    final, rest = compress(second)

    fin[...] = final
    f_copies = [
        remote(fin, gat.at[c, x, lax.rem(z, 2), y, z // 2], (f_s, f_r), d, (x, y, lax.rem(z + d, NZ), c)) for d in far_first
    ]
    gat[c, x, lax.rem(z, 2), y, z // 2] = final
    loads[11].wait()
    for i in range(4):
        rows = pl.ds(256 * i, 256)
        ig[rows, :] = lax.dot_general(
            cot[rows, :], w[...], (((1,), (1,)), ((), ())), preferred_element_type=F32
        ).astype(BF16)
    keep(ig, ig_h)
    cn[0:16, :] = rest[:, 0:64]
    cn[16:32, :] = pltpu.roll(rest, 64, axis=1)[:, 0:64]
    keep(cn, cn_h)
    nearest = sorted(
        [(dx, dy) for dx in range(NX) for dy in range(NY)],
        key=lambda d: min(d[0], NX - d[0]) + min(d[1], NY - d[1]),
    )
    p_copies, t_copies = {}, {}
    mine = z // 4

    def part_of(near):
        return pl.ds(2 * mine if near else 2 - 2 * mine, 2)

    def to_plane(near):
        block = gat.at[c, x, :, y, part_of(near)]
        for dx, dy in nearest[:0:-1]:
            there = (lax.rem(x + dx, NX), lax.rem(y + dy, NY), z, c)
            p_copies[near, dx, dy] = remote(block, block, (p_s, p_r), (near, dx, dy), there)

    def to_sibling(near, dx, dy):
        if dx or dy:
            p_copies[near, dx, dy].wait_recv()
        sx, sy = lax.rem(x - dx + NX, NX), lax.rem(y - dy + NY, NY)
        block = gat.at[c, sx, :, sy, part_of(near)]
        t_copies[near, dx, dy] = remote(block, block, (t_s, t_r), (near, dx, dy), (x, y, z, 1 - c))

    def unpack(dx):
        sx = lax.rem(x - dx + NX, NX)
        for h in range(2):
            for sy in range(NY):
                for i in range(NZ // 2):
                    halves = fold(gat[0, sx, h, sy, i], gat[1, sx, h, sy, i])
                    for side in range(2):
                        rows = pl.ds(256 * side + 4 * sy + i, 16, stride=ROWS)
                        avg[4 * h + sx, rows, :] = halves[side].astype(F32)
            keep(avg.at[4 * h + sx], avg_h.at[4 * h + sx])

    def piece_from(at):
        d = lax.rem(z - at + NZ, NZ)
        pltpu.make_async_remote_copy(
            src_ref=fin, dst_ref=gat.at[c, x, 0, y, 0], send_sem=f_s.at[d], recv_sem=f_r.at[d],
            device_id=device(x, y, lax.rem(z + d, NZ), c), device_id_type=MESH,
        ).wait_recv()

    finished(c_copies)
    for i in range(1, 4):
        piece_from(4 * mine + lax.rem(z + i, 4))
    to_plane(1)
    for i in range(4):
        piece_from(4 - 4 * mine + i)
    to_plane(0)
    finished(f_copies)
    for copy in outs[:4]:
        copy.wait()
    for at in nearest:
        to_sibling(1, *at)
    for at in nearest:
        to_sibling(0, *at)
    finished([p_copies[1, dx, dy] for dx, dy in nearest[1:]])
    for dx in (0, 1, 3, 2):
        for near in (1, 0):
            for dy in range(NY):
                t_copies[near, dx, dy].wait_recv()
        unpack(dx)
    finished([p_copies[0, dx, dy] for dx, dy in nearest[1:]] + [t_copies[1, dx, dy] for dx, dy in nearest])
    finished([t_copies[0, dx, dy] for dx, dy in nearest])
    for copy in outs[4:]:
        copy.wait()


def finish(avg, wn, ig, rn, cn, avg_out, wn_out, ig_out, rn_out, cn_out, sem):
    moves = [(ig, ig_out), (rn, rn_out.at[0, 0]), (cn, cn_out.at[0, 0])]
    moves += [(wn.at[q], wn_out.at[0, 0, :, pl.ds(1024 * q, 1024)]) for q in range(ROWS)]
    moves += [(avg.at[k], avg_out.at[:, pl.ds(128 * k, 128)]) for k in range(8)]
    copies = [pltpu.make_async_copy(src, dst, sem.at[i]) for i, (src, dst) in enumerate(moves)]
    for copy in copies:
        copy.start()
    for copy in copies:
        copy.wait()


def local(context, cotangent, out_weight, momentum, worker_error, server_rows, server_cols):
    anywhere = pl.BlockSpec(memory_space=pl.ANY)
    dma = pltpu.SemaphoreType.DMA
    args = (context, cotangent, out_weight, momentum, worker_error, server_rows, server_cols)
    held = pl.pallas_call(
        fused,
        out_shape=(
            pltpu.VMEM((8, 512, 128), F32),
            pltpu.VMEM((ROWS, LANES, 1024), F32),
            pltpu.VMEM((1024, 512), BF16),
            pltpu.VMEM((LANES, BLOCK), F32),
            pltpu.VMEM((LANES, 64), F32),
        ),
        in_specs=[anywhere] * 7,
        out_specs=[anywhere] * 5,
        scratch_shapes=[
            pltpu.VMEM((1024, 512), BF16),
            pltpu.VMEM((1024, 1024), BF16),
            pltpu.VMEM((512, 1024), BF16),
            pltpu.VMEM((8, 512, 128), F32),
            pltpu.VMEM((LANES, WIDTH), F32),
            pltpu.VMEM((LANES, BLOCK), F32),
            pltpu.VMEM((LANES, 64), F32),
            pltpu.VMEM((512, 1024), BF16),
            pltpu.VMEM((8, 512, 128), F32),
            pltpu.VMEM((8, 512, 128), F32),
            pltpu.VMEM((ROWS, LANES, 1024), F32),
            pltpu.VMEM((1024, 512), BF16),
            pltpu.VMEM((LANES, BLOCK), F32),
            pltpu.VMEM((LANES, 64), F32),
            pltpu.VMEM((NY, NZ, LANES, YC), BF16),
            pltpu.VMEM((NY, NZ, LANES, YC), BF16),
            pltpu.VMEM((NZ, NY, LANES, ZC), BF16),
            pltpu.VMEM((NZ, NY, LANES, ZC), BF16),
            pltpu.VMEM((NZ, LANES, YC), BF16),
            pltpu.VMEM((NZ, LANES, YC), BF16),
            pltpu.VMEM((NY, LANES, ZC), BF16),
            pltpu.VMEM((NY, LANES, ZC), BF16),
            pltpu.VMEM((NX * NC, 16, 128), BF16),
            pltpu.VMEM((NX * NC, 16, 128), BF16),
            pltpu.VMEM((16, 128), BF16),
            pltpu.VMEM((NC, NX, 2, NY, NZ // 2, 16, 128), BF16),
            dma((18,)), dma((12,)),
            dma((4, NY)), dma((4, NY)), dma((NZ,)), dma((NZ,)), dma((NZ,)), dma((NZ,)), dma((NY,)), dma((NY,)),
            dma((NX * NC,)), dma((NX * NC,)), dma((NZ,)), dma((NZ,)),
            dma((2, NX, NY)), dma((2, NX, NY)), dma((2, NX, NY)), dma((2, NX, NY)),
        ],
        compiler_params=pltpu.CompilerParams(
            collective_id=0, has_side_effects=True, vmem_limit_bytes=44 << 20
        ),
        cost_estimate=pl.CostEstimate(flops=2 << 30, bytes_accessed=13 << 20, transcendentals=1 << 19),
        name="fused",
    )(*[pltpu.with_memory_space_constraint(arg, pltpu.HBM) for arg in args])
    return pl.pallas_call(
        finish,
        out_shape=(
            jax.ShapeDtypeStruct((512, 1024), F32),
            jax.ShapeDtypeStruct((1, 1, LANES, WIDTH), F32),
            jax.ShapeDtypeStruct((1024, 512), BF16),
            jax.ShapeDtypeStruct((1, 1, LANES, BLOCK), F32),
            jax.ShapeDtypeStruct((1, 1, LANES, 64), F32),
        ),
        in_specs=[anywhere] * 5,
        out_specs=[anywhere] * 5,
        scratch_shapes=[dma((27,))],
        compiler_params=pltpu.CompilerParams(vmem_limit_bytes=16 << 20),
        cost_estimate=pl.CostEstimate(flops=0, bytes_accessed=5 << 20, transcendentals=0),
        name="finish",
    )(*held)


def solution(mesh):
    state = P("row", "col", None, None)
    tokens = P(("row", "col"), None)

    def body(*args):
        avg, wn, ig, rn, cn = local(*args)
        return ig, avg, wn, rn, cn

    return jax.shard_map(
        body,
        mesh=mesh,
        in_specs=(tokens, tokens, P(), P(), state, state, state),
        out_specs=(tokens, P(), state, state, state),
        check_vma=False,
    )
```
